32 devices in a mesh: shot: 8 (over z, x), line: 4 (over y, core).
Axes of the slice: x: 2, y: 2, z: 4, core: 2. Of those that a mesh axis runs over, the one named last changes fastest.
Arguments:
- data: bfloat16 [8, 8, 256, 1024], P('shot', 'line'), may hold values from -6 to 6
- live_mask: int32 [8, 8, 256], P('shot', 'line'), may hold values 0 or 1
- patch_start: int32 [8, 8], replicated, may hold values from 0 to 256
- receiver_slot: int32 [8, 512], P('line'), may hold values from 0 to 511, each once within a row
- shot_kernels: bfloat16 [6, 3, 5, 31], replicated, may hold values from -0.25 to 0.25
- shot_tau: float32 [6], replicated, may hold values from 0.2 to 2
- receiver_kernels: bfloat16 [6, 5, 31], replicated, may hold values from -0.5 to 0.5
- receiver_tau: float32 [6], replicated, may hold values from 0.2 to 2
Outputs:
- receiver_gathers: bfloat16 [8, 512, 8, 1024], P('line', 'shot')
The draws below stay inside these ranges and needn't reach their ends.
Inputs may be any that keep to these rules, and one draw needn't show every extreme that they name: Each row of receiver_slot names every slot once.
All inputs are finite; a program needn't handle non-finite values. No bound on the sum of `live_mask` on one device may be relied on, other than what follows from the above.
Results may differ from the reference program's by a relative error of at most 0.0051.
Values may be sent and summed in bfloat16 or wider, within the bound.
A program may use at most 192 MiB of HBM per device.

```python
import math
import jax
import jax.numpy as jnp
from jax import lax

LINES = 8
CH = 256
NT = 1024
KERN = 6
KERN2 = 6
TAPS = 31
SHOTS = 8
STATIONS = 512


def touch_ends(values, rng, low, top_value):
    longest = values.shape.index(max(values.shape))
    spots = []
    for shift in (0, 1):
        where = [jax.random.randint(jax.random.fold_in(rng, axis), (), 0, length) for axis, length in enumerate(values.shape)]
        where[longest] = (where[longest] + shift) % values.shape[longest]
        spots.append(tuple(where))
    return values.at[spots[0]].set(low).at[spots[1]].set(top_value)


def levels(own_key, extent, pieces, smallest, high):
    loudness, own = 1.0, jax.random.fold_in(own_key, 6)
    for axis_at, blocks in pieces:
        heights = jnp.exp(jax.random.uniform(jax.random.fold_in(own, axis_at), (blocks,), jnp.float32, smallest / len(pieces), high / len(pieces)))
        loudness = loudness * jnp.repeat(heights, extent[axis_at] // blocks).reshape([-1 if axis == axis_at else 1 for axis in range(len(extent))])
    return loudness


def scatter_about(rng, dims, width, limit, cuts=(), held_as=jnp.bfloat16):
    factor_of = levels(rng, dims, cuts, -0.22, 0.18) if cuts else 1.0
    drawn = jax.random.normal(rng, dims, jnp.float32) * width * factor_of
    return jnp.minimum(jnp.maximum(drawn, -limit), limit).astype(held_as)


def setup_inputs(seed: int = 0) -> dict:
    key_list = jax.random.split(jax.random.key(seed), 9)
    return {
        "data": scatter_about(key_list[0], (SHOTS, LINES, CH, NT), 1.0, 6.0, ((0, 8), (1, 4))),
        "live_mask": touch_ends((jax.random.randint(key_list[1], (SHOTS, LINES, CH), 0, 10) < 9).astype(jnp.int32), jax.random.fold_in(key_list[1], 1), 0, 1),
        "patch_start": touch_ends(jax.random.randint(key_list[2], (SHOTS, LINES), 0, CH + 1), jax.random.fold_in(key_list[2], 1), 0, CH).astype(jnp.int32),
        "receiver_slot": jax.vmap(lambda own: jax.random.permutation(own, STATIONS))(jax.random.split(key_list[3], LINES)).reshape((LINES, STATIONS)).astype(jnp.int32),
        "shot_kernels": scatter_about(key_list[4], (KERN, 3, 5, TAPS), (15 * TAPS) ** -0.5, 0.25),
        "shot_tau": jnp.clip(jnp.exp(jax.random.uniform(key_list[5], (KERN,), jnp.float32, math.log(0.2), math.log(2.0))), 0.2, 2.0),
        "receiver_kernels": scatter_about(key_list[6], (KERN2, 5, TAPS), (5 * TAPS) ** -0.5, 0.5),
        "receiver_tau": jnp.clip(jnp.exp(jax.random.uniform(key_list[7], (KERN2,), jnp.float32, math.log(0.2), math.log(2.0))), 0.2, 2.0),
    }


def shrink_sum(filtered, tau):
    tau_sq = (tau * tau).reshape((tau.shape[0],) + (1,) * (filtered.ndim - 1))
    return jnp.sum(filtered * filtered * filtered / (filtered * filtered + tau_sq), axis=0)


def reference(data, live_mask, patch_start, receiver_slot, shot_kernels, shot_tau, receiver_kernels, receiver_tau):
    mask_f = live_mask.astype(jnp.float32)
    kernels_one = shot_kernels.astype(jnp.float32)[:, None]
    kernels_two = receiver_kernels.astype(jnp.float32)[:, None]

    def section_one(pair):
        shot_data, shot_mask = pair
        live_data = shot_data.astype(jnp.float32) * shot_mask[..., None]
        filtered = lax.conv_general_dilated(live_data[None, None], kernels_one, (1, 1, 1), [(1, 1), (2, 2), (15, 15)], dimension_numbers=("NCDHW", "OIDHW", "NCDHW"), precision=lax.Precision.HIGHEST)[0]
        noise_est = shrink_sum(filtered, shot_tau)
        return ((live_data - noise_est) * shot_mask[..., None]).astype(jnp.bfloat16)

    cleaned = lax.map(section_one, (data, mask_f))
    station_ids = jnp.arange(STATIONS, dtype=jnp.int32)
    fold_ids = jnp.arange(SHOTS, dtype=jnp.int32)

    def section_two(triple):
        traces, start_cols, slots = triple
        channel = station_ids[None, :] - start_cols[:, None]
        covered = (channel >= 0) & (channel < CH)
        clipped = jnp.clip(channel, 0, CH - 1).astype(jnp.int32)
        grid = jnp.take_along_axis(traces, clipped[:, :, None], axis=1).astype(jnp.float32)
        fold = jnp.cumsum(covered.astype(jnp.int32), axis=0) - 1
        fold = jnp.where(covered, fold, -1)
        onehot = (fold[:, :, None] == fold_ids[None, None, :]).astype(jnp.float32)
        gathered = jnp.einsum("srf,srt->rft", onehot, grid, precision=lax.Precision.HIGHEST)
        count = jnp.sum(covered.astype(jnp.int32), axis=0)
        live_fold = (fold_ids[None, :] < count[:, None]).astype(jnp.float32)
        filtered = lax.conv_general_dilated(gathered[:, None], kernels_two, (1, 1), [(2, 2), (15, 15)], dimension_numbers=("NCHW", "OIHW", "NCHW"), precision=lax.Precision.HIGHEST)
        filtered = jnp.transpose(filtered, (1, 0, 2, 3))
        noise_est = shrink_sum(filtered, receiver_tau)
        result = ((gathered - noise_est) * live_fold[:, :, None]).astype(jnp.bfloat16)
        slot_station = jnp.zeros((STATIONS,), jnp.int32).at[slots].set(station_ids)
        return result[slot_station]

    by_line = jnp.transpose(cleaned, (1, 0, 2, 3))
    return lax.map(section_two, (by_line, jnp.transpose(patch_start), receiver_slot))
```

```python
import functools

import jax
import jax.numpy as jnp
from jax import lax
from jax.experimental import pallas as pl
from jax.experimental.pallas import tpu as pltpu
from jax.sharding import PartitionSpec as P

BF = jnp.bfloat16
F32 = jnp.float32
STEP_ONE = 32
STEP_TWO = 16
VMEM = 58 * 1024 * 1024


def band_matrix(kernels, step, chunks):
    bank, taps = kernels.shape[0], kernels.shape[-1]
    flat = kernels.reshape(bank, -1, taps)
    out_pos = jnp.arange(step, dtype=jnp.int32)[:, None, None]
    in_pos = jnp.arange(step * chunks, dtype=jnp.int32)[None, :, None]
    tap = jnp.arange(taps, dtype=jnp.int32)[None, None, :]
    lead = 16 - taps // 2
    onehot = (in_pos - out_pos - lead == tap).astype(BF).reshape(step, chunks, step, taps)
    band = jnp.einsum("kot,ujrt->kujor", flat, onehot, preferred_element_type=F32)
    return band.astype(BF).reshape(bank * step, -1)


def nt_dot(a, b):
    return lax.dot_general(a, b, (((1,), (1,)), ((), ())), preferred_element_type=F32)


def shrink(filtered, tau_ref, bank, step):
    total = None
    for k in range(bank):
        f = filtered[k * step : (k + 1) * step]
        sq = f * f
        tau = tau_ref[k]
        term = (f * sq) * pl.reciprocal(sq + tau * tau, approx=True)
        total = term if total is None else total + term
    return total


def shot_kernel(live_ref, top_ref, bottom_ref, mask_ref, band_ref, tau_ref, row_ref, out_ref, wins, clean, pick):
    lines, channels, samples = live_ref.shape
    step = STEP_ONE
    blocks = samples // step
    bank = tau_ref.shape[0]
    depth = 5 * step
    src = lax.broadcasted_iota(jnp.int32, (channels, channels), 0)
    dst = lax.broadcasted_iota(jnp.int32, (channels, channels), 1)
    shifts = [jnp.where(src == dst + (b - 2), 1.0, 0.0).astype(BF) for b in range(5)]
    zeros = jnp.zeros((16, channels), BF)
    for n in range(lines + 2):
        for b in range(5):
            base = n * depth + b * step
            wins[0, base : base + 16, :] = zeros
            wins[blocks, base + 16 : base + 32, :] = zeros

    per = 128 // step
    for n in range(lines + 2):
        ref = top_ref.at[0] if n == 0 else bottom_ref.at[0] if n == lines + 1 else live_ref.at[n - 1]

        def spread(m, carry, n=n, ref=ref):
            cols = pl.ds(pl.multiple_of(m * 128, 128), 128)
            turned = ref[:, cols].astype(F32).T.astype(BF)
            for b in range(5):
                base = n * depth + b * step
                if b == 2:
                    moved = turned
                else:
                    moved = jnp.dot(turned, shifts[b], preferred_element_type=F32).astype(BF)
                wins[m * per, base + 16 : base + 32, :] = moved[0:16]
                for q in range(1, per):
                    wins[m * per + q, base : base + 32, :] = moved[q * 32 - 16 : q * 32 + 16]
                wins[m * per + per, base : base + 16, :] = moved[112:128]
            return carry

        lax.fori_loop(0, samples // 128, spread, 0)

    half = 3 * depth

    def block(j, carry):
        for n in range(lines):
            lo = n * depth
            filtered = jnp.dot(band_ref[:, :half], wins[j, lo : lo + half, :], preferred_element_type=F32)
            filtered += jnp.dot(band_ref[:, half:], wins[j + 1, lo : lo + half, :], preferred_element_type=F32)
            noise = shrink(filtered, tau_ref, bank, step)
            mid = lo + depth + 2 * step
            live = jnp.concatenate(
                [wins[j, mid + 16 : mid + 32, :].astype(F32), wins[j + 1, mid : mid + 16, :].astype(F32)], axis=0
            )
            kept = (live - noise) * mask_ref[n : n + 1, :]
            clean[pl.ds(pl.multiple_of(j * step, step), step), n * channels : (n + 1) * channels] = kept.astype(BF)
        return carry

    lax.fori_loop(0, blocks, block, 0)

    rows = out_ref.shape[0]
    spot = lax.broadcasted_iota(jnp.int32, (rows, lines * channels), 0)
    pick[...] = jnp.where(spot == row_ref[...], 1.0, 0.0).astype(BF)

    def route(m, carry):
        span = pl.ds(pl.multiple_of(m * 256, 256), 256)
        out_ref[:, span] = nt_dot(pick[...], clean[span, :]).astype(BF)
        return carry

    lax.fori_loop(0, samples // 256, route, 0)


def receiver_kernel(folds, got_ref, spot_ref, band_ref, tau_ref, out_ref, wins, done, place, perm):
    rows, samples = got_ref.shape
    width = spot_ref.shape[1]
    fold_lanes = width // folds
    step = STEP_TWO
    blocks = samples // step
    bank = tau_ref.shape[0]
    depth = 5 * step
    aligned = fold_lanes % 128 == 0
    wins[0] = jnp.zeros((depth, width), BF)
    wins[blocks + 1] = jnp.zeros((depth, width), BF)
    ids = lax.broadcasted_iota(jnp.int32, (rows, width), 0)
    for b in [2] if aligned else range(5):
        place[0 if aligned else b] = jnp.where(ids == spot_ref[b : b + 1, :], 1.0, 0.0).astype(BF)
    out_id = lax.broadcasted_iota(jnp.int32, (width, width), 0)
    lane = lax.broadcasted_iota(jnp.int32, (width, width), 1)
    perm[...] = jnp.where((out_id % folds) * fold_lanes + out_id // folds == lane, 1.0, 0.0).astype(BF)
    per = 128 // step

    def assemble(m, carry):
        cols = pl.ds(pl.multiple_of(m * 128, 128), 128)
        turned = got_ref[:, cols].astype(F32).T.astype(BF)
        at = pl.ds(m * per + 1, per)
        if aligned:
            cells = jnp.dot(turned, place[0], preferred_element_type=F32).astype(BF)
            cells = cells.reshape(per, step, width)
            for b in range(5):
                gap = (b - 2) * fold_lanes
                lo, hi = max(0, -gap), width - max(0, gap)
                r = slice(b * step, (b + 1) * step)
                wins[at, r, lo:hi] = cells[:, :, lo + gap : hi + gap]
                if lo > 0:
                    wins[at, r, 0:lo] = jnp.zeros((per, step, lo), BF)
                if hi < width:
                    wins[at, r, hi:width] = jnp.zeros((per, step, width - hi), BF)
        else:
            for b in range(5):
                cells = jnp.dot(turned, place[b], preferred_element_type=F32).astype(BF)
                wins[at, b * step : (b + 1) * step, :] = cells.reshape(per, step, width)
        return carry

    lax.fori_loop(0, samples // 128, assemble, 0)

    def block(j, carry):
        for g in range(width // 256):
            lanes = slice(g * 256, (g + 1) * 256)
            stack = wins[pl.ds(j, 3), :, lanes].reshape(3 * depth, 256)
            filtered = jnp.dot(band_ref[...], stack, preferred_element_type=F32)
            noise = shrink(filtered, tau_ref, bank, step)
            centre = wins[j + 1, 2 * step : 3 * step, lanes].astype(F32)
            mask = jnp.where(spot_ref[2:3, lanes] >= 0, 1.0, 0.0)
            done[pl.ds(pl.multiple_of(j * step, step), step), lanes] = ((centre - noise) * mask).astype(BF)
        return carry

    lax.fori_loop(0, blocks, block, 0)

    def restore(m, carry):
        span = pl.ds(pl.multiple_of(m * 256, 256), 256)
        turned = nt_dot(perm[...], done[span, :])
        out_ref[:, :, span] = turned.reshape(fold_lanes, folds, 256).astype(BF)
        return carry

    lax.fori_loop(0, samples // 256, restore, 0)


def vmem():
    return pl.BlockSpec(memory_space=pltpu.VMEM)


def smem():
    return pl.BlockSpec(memory_space=pltpu.SMEM)


def per_device(
    data, live_mask, patch_start, receiver_slot, shot_kernels, shot_tau, receiver_kernels, receiver_tau
):
    _, lines, channels, samples = data.shape
    stations = receiver_slot.shape[1]
    shots = patch_start.shape[0]
    owners = lax.axis_size("shot")
    slots = stations // owners
    me = lax.axis_index("shot")
    first_line = lax.axis_index("line") * lines
    ends = lax.axis_size("line") - 1
    fold_lanes = lines * slots
    width = shots * fold_lanes
    capacity = fold_lanes

    mask = live_mask[0]
    live = data[0] * mask[..., None].astype(BF)
    top = lax.ppermute(live[lines - 1 :], "line", [(i, i + 1) for i in range(ends)])
    bottom = lax.ppermute(live[:1], "line", [(i + 1, i) for i in range(ends)])

    band_one = band_matrix(shot_kernels, STEP_ONE, 2)
    band_two = band_matrix(receiver_kernels, STEP_TWO, 3)

    starts = lax.dynamic_slice_in_dim(patch_start, first_line, lines, 1)
    own_starts = lax.dynamic_slice_in_dim(starts, me, 1, 0)[0]
    own_slots = jnp.concatenate(
        [lax.dynamic_slice(receiver_slot, (n, own_starts[n]), (1, channels)) for n in range(lines)], axis=0
    )
    owner = own_slots // slots
    line_ids = jnp.arange(lines, dtype=jnp.int32)[:, None]
    rows = owner * capacity + line_ids * slots + own_slots % slots
    rows = rows.reshape(1, lines * channels)
    slot_ids = me * slots + jnp.arange(slots, dtype=jnp.int32)
    hits = receiver_slot[:, None, :] == slot_ids[None, :, None]
    station = jnp.sum(jnp.where(hits, jnp.arange(stations, dtype=jnp.int32), 0), axis=-1)
    channel = station[None] - starts[:, :, None]
    covered = (channel >= 0) & (channel < channels)
    covered = covered.reshape(shots, fold_lanes)
    before = jnp.tril(jnp.ones((shots, shots), jnp.int32), -1)
    fold = jnp.sum(before[:, :, None] * covered[None].astype(jnp.int32), axis=1)
    source = jnp.arange(shots, dtype=jnp.int32)[:, None] * capacity + jnp.arange(fold_lanes, dtype=jnp.int32)[None]
    fold_ids = jnp.arange(shots, dtype=jnp.int32)[:, None, None]
    spot = jnp.sum(jnp.where(covered[None] & (fold[None] == fold_ids), source[None] + 1, 0), axis=1) - 1
    spot = spot.reshape(width)
    padded = jnp.pad(spot, (2 * fold_lanes, 2 * fold_lanes), constant_values=-1)
    spots = jnp.stack([padded[b * fold_lanes : b * fold_lanes + width] for b in range(5)])

    blocks = samples // STEP_ONE
    send = pl.pallas_call(
        shot_kernel,
        out_shape=jax.ShapeDtypeStruct((owners * capacity, samples), BF),
        in_specs=[vmem(), vmem(), vmem(), vmem(), vmem(), smem(), vmem()],
        out_specs=vmem(),
        scratch_shapes=[
            pltpu.VMEM((blocks + 1, (lines + 2) * 5 * STEP_ONE, channels), BF),
            pltpu.VMEM((samples, lines * channels), BF),
            pltpu.VMEM((owners * capacity, lines * channels), BF),
        ],
        compiler_params=pltpu.CompilerParams(vmem_limit_bytes=VMEM),
        name="shot_bank",
    )(live, top, bottom, mask.astype(F32), band_one, shot_tau, rows)

    got = lax.all_to_all(send.reshape(owners, capacity, samples), "shot", split_axis=0, concat_axis=0, tiled=True)
    got = got.reshape(shots * capacity, samples)

    count = 1 if fold_lanes % 128 == 0 else 5
    out = pl.pallas_call(
        functools.partial(receiver_kernel, shots),
        out_shape=jax.ShapeDtypeStruct((fold_lanes, shots, samples), BF),
        in_specs=[vmem(), vmem(), vmem(), smem()],
        out_specs=vmem(),
        scratch_shapes=[
            pltpu.VMEM((samples // STEP_TWO + 2, 5 * STEP_TWO, width), BF),
            pltpu.VMEM((samples, width), BF),
            pltpu.VMEM((count, shots * capacity, width), BF),
            pltpu.VMEM((width, width), BF),
        ],
        compiler_params=pltpu.CompilerParams(vmem_limit_bytes=VMEM),
        name="receiver_bank",
    )(got, spots, band_two, receiver_tau)
    return out.reshape(lines, slots, shots, samples)


def solution(mesh):
    return jax.shard_map(
        per_device,
        mesh=mesh,
        in_specs=(
            P("shot", "line", None, None),
            P("shot", "line", None),
            P(),
            P("line", None),
            P(),
            P(),
            P(),
            P(),
        ),
        out_specs=P("line", "shot", None, None),
        check_vma=False,
    )
```

```python
import functools
import math

import jax
import jax.numpy as jnp
from jax import lax
from jax.experimental import pallas as pl
from jax.experimental.pallas import tpu as pltpu
from jax.sharding import PartitionSpec as P

BF = jnp.bfloat16
F32 = jnp.float32
STEP_ONE = 32
STEP_TWO = 16
CHUNKS = 4
VMEM = 58 * 1024 * 1024


def band_matrix(kernels, step, chunks):
    bank, taps = kernels.shape[0], kernels.shape[-1]
    flat = kernels.reshape(bank, -1, taps)
    out_pos = jnp.arange(step, dtype=jnp.int32)[:, None, None]
    in_pos = jnp.arange(step * chunks, dtype=jnp.int32)[None, :, None]
    tap = jnp.arange(taps, dtype=jnp.int32)[None, None, :]
    lead = 16 - taps // 2
    onehot = (in_pos - out_pos - lead == tap).astype(BF).reshape(step, chunks, step, taps)
    band = jnp.einsum("kot,ujrt->kujor", flat, onehot, preferred_element_type=F32)
    return band.astype(BF).reshape(bank * step, -1)


def nt_dot(a, b):
    return lax.dot_general(a, b, (((1,), (1,)), ((), ())), preferred_element_type=F32)


def shrink(filtered, tau_ref, bank, step):
    total = None
    for k in range(bank):
        f = filtered[k * step : (k + 1) * step]
        sq = f * f
        tau = tau_ref[k]
        term = (f * sq) * pl.reciprocal(sq + tau * tau, approx=True)
        total = term if total is None else total + term
    return total


def bank_kernel(
    folds, live_ref, top_ref, bottom_ref, mask_ref, row_ref, spot_ref, band_one, tau_one, band_two, tau_two,
    out_ref, wins, clean, pick, send, recv, cells_win, done, place, perm, send_sem, recv_sem,
):
    lines, channels, samples = live_ref.shape
    chunks, rows, span = send.shape
    owners = lax.axis_size("shot")
    me = lax.axis_index("shot")
    capacity = rows // owners
    width = spot_ref.shape[1]
    fold_lanes = width // folds
    aligned = fold_lanes % 128 == 0

    barrier = pltpu.get_barrier_semaphore()
    for k in range(1, owners):
        pl.semaphore_signal(
            barrier, inc=1, device_id={"shot": lax.rem(me + k, owners)}, device_id_type=pl.DeviceIdType.MESH
        )

    step = STEP_ONE
    blocks = samples // step
    bank = tau_one.shape[0]
    depth = 5 * step
    half = 3 * depth
    per = 128 // step
    tiles = span // 128
    src = lax.broadcasted_iota(jnp.int32, (channels, channels), 0)
    dst = lax.broadcasted_iota(jnp.int32, (channels, channels), 1)
    shifts = [jnp.where(src == dst + (b - 2), 1.0, 0.0).astype(BF) for b in range(5)]
    zeros = jnp.zeros((16, channels), BF)
    for n in range(lines + 2):
        for b in range(5):
            base = n * depth + b * step
            wins[0, base : base + 16, :] = zeros
            wins[blocks, base + 16 : base + 32, :] = zeros
    spot = lax.broadcasted_iota(jnp.int32, (rows, lines * channels), 0)
    pick[...] = jnp.where(spot == row_ref[...], 1.0, 0.0).astype(BF)

    def spread(m, carry):
        cols = pl.ds(pl.multiple_of(m * 128, 128), 128)
        for n in range(lines + 2):
            ref = top_ref.at[0] if n == 0 else bottom_ref.at[0] if n == lines + 1 else live_ref.at[n - 1]
            turned = ref[:, cols].astype(F32).T.astype(BF)
            for b in range(5):
                base = n * depth + b * step
                if b == 2:
                    moved = turned
                else:
                    moved = jnp.dot(turned, shifts[b], preferred_element_type=F32).astype(BF)
                wins[m * per, base + 16 : base + 32, :] = moved[0:16]
                for q in range(1, per):
                    wins[m * per + q, base : base + 32, :] = moved[q * 32 - 16 : q * 32 + 16]
                wins[m * per + per, base : base + 16, :] = moved[112:128]
        return carry

    def block_one(j, carry):
        for n in range(lines):
            lo = n * depth
            filtered = jnp.dot(band_one[:, :half], wins[j, lo : lo + half, :], preferred_element_type=F32)
            filtered += jnp.dot(band_one[:, half:], wins[j + 1, lo : lo + half, :], preferred_element_type=F32)
            noise = shrink(filtered, tau_one, bank, step)
            mid = lo + depth + 2 * step
            live = jnp.concatenate(
                [wins[j, mid + 16 : mid + 32, :].astype(F32), wins[j + 1, mid : mid + 16, :].astype(F32)], axis=0
            )
            kept = (live - noise) * mask_ref[n : n + 1, :]
            clean[pl.ds(pl.multiple_of(j * step, step), step), n * channels : (n + 1) * channels] = kept.astype(BF)
        return carry

    def copy(i, k):
        to = lax.rem(me + k, owners)
        return pltpu.make_async_remote_copy(
            src_ref=send.at[i, pl.ds(pl.multiple_of(to * capacity, 16), capacity), :],
            dst_ref=recv.at[i, pl.ds(pl.multiple_of(me * capacity, 16), capacity), :],
            send_sem=send_sem.at[i, k],
            recv_sem=recv_sem.at[i, k],
            device_id={"shot": to},
            device_id_type=pl.DeviceIdType.MESH,
        )

    def chunk_one(i, carry):
        later = (i + chunks - 1) // chunks
        last = i // (chunks - 1)
        lax.fori_loop(tiles * i + later, tiles * (i + 1) + 1 - last, spread, 0)
        lax.fori_loop(i * (span // step), (i + 1) * (span // step), block_one, 0)
        at = pl.ds(pl.multiple_of(i * span, span), span)
        send[i] = nt_dot(pick[...], clean[at, :]).astype(BF)
        for k in range(1, owners):
            copy(i, k).start()
        own = pl.ds(pl.multiple_of(me * capacity, 16), capacity)
        recv[i, own, :] = send[i, own, :]
        return carry

    pl.semaphore_wait(barrier, owners - 1)
    lax.fori_loop(0, chunks, chunk_one, 0)

    step_two = STEP_TWO
    blocks_two = samples // step_two
    bank_two = tau_two.shape[0]
    depth_two = 5 * step_two
    cells_win[0] = jnp.zeros((depth_two, width), BF)
    cells_win[blocks_two + 1] = jnp.zeros((depth_two, width), BF)
    ids = lax.broadcasted_iota(jnp.int32, (rows, width), 0)
    for b in [2] if aligned else range(5):
        place[0 if aligned else b] = jnp.where(ids == spot_ref[b : b + 1, :], 1.0, 0.0).astype(BF)
    out_id = lax.broadcasted_iota(jnp.int32, (width, width), 0)
    lane = lax.broadcasted_iota(jnp.int32, (width, width), 1)
    perm[...] = jnp.where((out_id % folds) * fold_lanes + out_id // folds == lane, 1.0, 0.0).astype(BF)
    per_two = 128 // step_two

    def assemble(i, tile):
        turned = recv[i, :, tile * 128 : (tile + 1) * 128].astype(F32).T.astype(BF)
        at = pl.ds((i * tiles + tile) * per_two + 1, per_two)
        if aligned:
            cells = jnp.dot(turned, place[0], preferred_element_type=F32).astype(BF)
            cells = cells.reshape(per_two, step_two, width)
            for b in range(5):
                gap = (b - 2) * fold_lanes
                lo, hi = max(0, -gap), width - max(0, gap)
                r = slice(b * step_two, (b + 1) * step_two)
                cells_win[at, r, lo:hi] = cells[:, :, lo + gap : hi + gap]
                if lo > 0:
                    cells_win[at, r, 0:lo] = jnp.zeros((per_two, step_two, lo), BF)
                if hi < width:
                    cells_win[at, r, hi:width] = jnp.zeros((per_two, step_two, width - hi), BF)
        else:
            for b in range(5):
                cells = jnp.dot(turned, place[b], preferred_element_type=F32).astype(BF)
                cells_win[at, b * step_two : (b + 1) * step_two, :] = cells.reshape(per_two, step_two, width)

    def block_two(j, carry):
        for g in range(width // 256):
            lanes = slice(g * 256, (g + 1) * 256)
            stack = cells_win[pl.ds(j, 3), :, lanes].reshape(3 * depth_two, 256)
            filtered = jnp.dot(band_two[...], stack, preferred_element_type=F32)
            noise = shrink(filtered, tau_two, bank_two, step_two)
            centre = cells_win[j + 1, 2 * step_two : 3 * step_two, lanes].astype(F32)
            mask = jnp.where(spot_ref[2:3, lanes] >= 0, 1.0, 0.0)
            at = pl.ds(pl.multiple_of(j * step_two, step_two), step_two)
            done[at, lanes] = ((centre - noise) * mask).astype(BF)
        return carry

    def restore(m, carry):
        at = pl.ds(pl.multiple_of(m * 128, 128), 128)
        turned = nt_dot(perm[...], done[at, :])
        out_ref[:, :, at] = turned.reshape(fold_lanes, folds, 128).astype(BF)
        return carry

    def chunk_two(i, carry):
        later = (i + chunks - 1) // chunks
        last = i // (chunks - 1)
        for k in range(1, owners):
            copy(i, k).wait_recv()
        for tile in range(tiles):
            assemble(i, tile)
        count = span // step_two
        lax.fori_loop(i * count - later, (i + 1) * count - 1 + last, block_two, 0)
        lax.fori_loop(i * tiles - later, (i + 1) * tiles - 1 + last, restore, 0)
        return carry

    lax.fori_loop(0, chunks, chunk_two, 0)

    def finish(i, carry):
        for k in range(1, owners):
            copy(i, k).wait_send()
        return carry

    lax.fori_loop(0, chunks, finish, 0)


def packed_rows(lines, slots, channels, stations):
    share = channels / stations
    room = 5.5 * math.sqrt(lines * slots * share * (1 - share))
    return min(lines * slots, -(-int(lines * slots * share + room) // 16) * 16)


def vmem():
    return pl.BlockSpec(memory_space=pltpu.VMEM)


def smem():
    return pl.BlockSpec(memory_space=pltpu.SMEM)


def per_device(
    data, live_mask, patch_start, receiver_slot, shot_kernels, shot_tau, receiver_kernels, receiver_tau
):
    _, lines, channels, samples = data.shape
    stations = receiver_slot.shape[1]
    shots = patch_start.shape[0]
    owners = lax.axis_size("shot")
    slots = stations // owners
    me = lax.axis_index("shot")
    first_line = lax.axis_index("line") * lines
    ends = lax.axis_size("line") - 1
    fold_lanes = lines * slots
    width = shots * fold_lanes
    capacity = packed_rows(lines, slots, channels, stations)

    mask = live_mask[0]
    live = data[0] * mask[..., None].astype(BF)
    top = lax.ppermute(live[lines - 1 :], "line", [(i, i + 1) for i in range(ends)])
    bottom = lax.ppermute(live[:1], "line", [(i + 1, i) for i in range(ends)])

    starts = lax.dynamic_slice_in_dim(patch_start, first_line, lines, 1)
    own_starts = lax.dynamic_slice_in_dim(starts, me, 1, 0)[0]
    own_slots = jnp.concatenate(
        [lax.dynamic_slice(receiver_slot, (n, own_starts[n]), (1, channels)) for n in range(lines)], axis=0
    )
    owner = (own_slots // slots).reshape(-1)
    line_ids = jnp.arange(lines, dtype=jnp.int32)[:, None]
    place = (line_ids * slots + own_slots % slots).reshape(-1)
    ahead = (owner[:, None] == owner[None, :]) & (place[None, :] < place[:, None])
    rank = jnp.sum(ahead.astype(jnp.int32), axis=1)
    slot_ids = me * slots + jnp.arange(slots, dtype=jnp.int32)
    hits = receiver_slot[:, None, :] == slot_ids[None, :, None]
    station = jnp.sum(jnp.where(hits, jnp.arange(stations, dtype=jnp.int32), 0), axis=-1)
    channel = station[None] - starts[:, :, None]
    covered = (channel >= 0) & (channel < channels)
    covered = covered.reshape(shots, fold_lanes)
    lower = jnp.tril(jnp.ones((shots, shots), jnp.int32), -1)
    fold = jnp.sum(lower[:, :, None] * covered[None].astype(jnp.int32), axis=1)
    before = jnp.tril(jnp.ones((fold_lanes, fold_lanes), jnp.int32), -1)
    order = jnp.sum(before[None] * covered[:, None, :].astype(jnp.int32), axis=2)
    fold_ids = jnp.arange(shots, dtype=jnp.int32)[:, None, None]
    takes = covered[None] & (fold[None] == fold_ids)
    shot_ids = jnp.arange(shots, dtype=jnp.int32)[:, None]

    band_one = band_matrix(shot_kernels, STEP_ONE, 2)
    band_two = band_matrix(receiver_kernels, STEP_TWO, 3)
    blocks = samples // STEP_ONE
    copies = 1 if fold_lanes % 128 == 0 else 5
    weights = mask.astype(F32)

    def run(size, ident):
        rows = jnp.where(rank < size, owner * size + rank, -1).reshape(1, lines * channels)
        source = shot_ids * size + order
        spot = (jnp.sum(jnp.where(takes, source[None] + 1, 0), axis=1) - 1).reshape(width)
        padded = jnp.pad(spot, (2 * fold_lanes, 2 * fold_lanes), constant_values=-1)
        spots = jnp.stack([padded[b * fold_lanes : b * fold_lanes + width] for b in range(5)])
        total = owners * size
        return pl.pallas_call(
            functools.partial(bank_kernel, shots),
            out_shape=jax.ShapeDtypeStruct((fold_lanes, shots, samples), BF),
            in_specs=[vmem()] * 7 + [smem(), vmem(), smem()],
            out_specs=vmem(),
            scratch_shapes=[
                pltpu.VMEM((blocks + 1, (lines + 2) * 5 * STEP_ONE, channels), BF),
                pltpu.VMEM((samples, lines * channels), BF),
                pltpu.VMEM((total, lines * channels), BF),
                pltpu.VMEM((CHUNKS, total, samples // CHUNKS), BF),
                pltpu.VMEM((CHUNKS, total, samples // CHUNKS), BF),
                pltpu.VMEM((samples // STEP_TWO + 2, 5 * STEP_TWO, width), BF),
                pltpu.VMEM((samples, width), BF),
                pltpu.VMEM((copies, total, width), BF),
                pltpu.VMEM((width, width), BF),
                pltpu.SemaphoreType.DMA((CHUNKS, owners)),
                pltpu.SemaphoreType.DMA((CHUNKS, owners)),
            ],
            compiler_params=pltpu.CompilerParams(
                vmem_limit_bytes=VMEM, collective_id=ident, has_side_effects=True
            ),
            name="banks",
        )(live, top, bottom, weights, rows, spots, band_one, shot_tau, band_two, receiver_tau)

    if capacity == fold_lanes:
        out = run(fold_lanes, 0)
    else:
        all_channels = jnp.arange(stations, dtype=jnp.int32)[None, None, :] - starts[:, :, None]
        lit = (all_channels >= 0) & (all_channels < channels)
        of_owner = receiver_slot[None] // slots == jnp.arange(owners, dtype=jnp.int32)[:, None, None]
        most = jnp.max(jnp.sum((lit[:, None] & of_owner[None]).astype(jnp.int32), axis=(2, 3)))
        most = lax.pmax(most, "line")
        out = lax.cond(most > capacity, lambda: run(fold_lanes, 0), lambda: run(capacity, 1))
    return out.reshape(lines, slots, shots, samples)


def solution(mesh):
    return jax.shard_map(
        per_device,
        mesh=mesh,
        in_specs=(
            P("shot", "line", None, None),
            P("shot", "line", None),
            P(),
            P("line", None),
            P(),
            P(),
            P(),
            P(),
        ),
        out_specs=P("line", "shot", None, None),
        check_vma=False,
    )
```

```python
import functools

import jax
import jax.numpy as jnp
import numpy as np
from jax import lax
from jax.experimental import pallas as pl
from jax.experimental.pallas import tpu as pltpu
from jax.sharding import PartitionSpec as P

BF = jnp.bfloat16
F32 = jnp.float32
STEP_ONE = 32
STEP_TWO = 16
CHUNKS = 8
VMEM = 58 * 1024 * 1024


def band_matrix(kernels, step, chunks):
    bank, taps = kernels.shape[0], kernels.shape[-1]
    flat = kernels.reshape(bank, -1, taps)
    out_pos = np.arange(step)[:, None, None]
    in_pos = np.arange(step * chunks)[None, :, None]
    tap = np.arange(taps)[None, None, :]
    lead = 16 - taps // 2
    onehot = jnp.asarray((in_pos - out_pos - lead == tap).reshape(step, chunks, step, taps), BF)
    band = jnp.einsum("kot,ujrt->kujor", flat, onehot, preferred_element_type=F32)
    return band.astype(BF).reshape(bank * step, -1)


def nt_dot(a, b):
    return lax.dot_general(a, b, (((1,), (1,)), ((), ())), preferred_element_type=F32)


def shrink(filtered, tau_ref, bank, step):
    total = None
    for k in range(bank):
        f = filtered[k * step : (k + 1) * step]
        sq = f * f
        tau = tau_ref[k]
        term = (f * sq) * pl.reciprocal(sq + tau * tau, approx=True)
        total = term if total is None else total + term
    return total


def bank_kernel(
    folds, live_ref, top_ref, bottom_ref, mask_ref, row_ref, spot_ref, band_one, tau_one, band_two, tau_two,
    out_ref, wins, clean, pick, send, recv, cells_win, done, place, perm, send_sem, recv_sem,
):
    lines, channels, samples = live_ref.shape
    chunks, rows, span = send.shape
    owners = lax.axis_size("shot")
    me = lax.axis_index("shot")
    capacity = rows // owners
    width = spot_ref.shape[1]
    fold_lanes = width // folds
    aligned = fold_lanes % 128 == 0

    barrier = pltpu.get_barrier_semaphore()
    for k in range(1, owners):
        pl.semaphore_signal(
            barrier, inc=1, device_id={"shot": lax.rem(me + k, owners)}, device_id_type=pl.DeviceIdType.MESH
        )

    step = STEP_ONE
    blocks = samples // step
    bank = tau_one.shape[0]
    depth = 5 * step
    half = 3 * depth
    per = 128 // step
    tiles = span // 128
    src = lax.broadcasted_iota(jnp.int32, (channels, channels), 0)
    dst = lax.broadcasted_iota(jnp.int32, (channels, channels), 1)
    shifts = [jnp.where(src == dst + (b - 2), 1.0, 0.0).astype(BF) for b in range(5)]
    zeros = jnp.zeros((16, channels), BF)
    for n in range(lines + 2):
        for b in range(5):
            base = n * depth + b * step
            wins[0, base : base + 16, :] = zeros
            wins[blocks, base + 16 : base + 32, :] = zeros
    spot = lax.broadcasted_iota(jnp.int32, (rows, lines * channels), 0)
    pick[...] = jnp.where(spot == row_ref[...], 1.0, 0.0).astype(BF)

    def spread(m, carry):
        cols = pl.ds(pl.multiple_of(m * 128, 128), 128)
        for n in range(lines + 2):
            ref = top_ref.at[0] if n == 0 else bottom_ref.at[0] if n == lines + 1 else live_ref.at[n - 1]
            turned = ref[:, cols].astype(F32).T.astype(BF)
            for b in range(5):
                base = n * depth + b * step
                if b == 2:
                    moved = turned
                else:
                    moved = jnp.dot(turned, shifts[b], preferred_element_type=F32).astype(BF)
                wins[m * per, base + 16 : base + 32, :] = moved[0:16]
                for q in range(1, per):
                    wins[m * per + q, base : base + 32, :] = moved[q * 32 - 16 : q * 32 + 16]
                wins[m * per + per, base : base + 16, :] = moved[112:128]
        return carry

    def block_one(j, carry):
        for n in range(lines):
            lo = n * depth
            filtered = jnp.dot(band_one[:, :half], wins[j, lo : lo + half, :], preferred_element_type=F32)
            filtered += jnp.dot(band_one[:, half:], wins[j + 1, lo : lo + half, :], preferred_element_type=F32)
            noise = shrink(filtered, tau_one, bank, step)
            mid = lo + depth + 2 * step
            live = jnp.concatenate(
                [wins[j, mid + 16 : mid + 32, :].astype(F32), wins[j + 1, mid : mid + 16, :].astype(F32)], axis=0
            )
            kept = (live - noise) * mask_ref[n : n + 1, :]
            clean[pl.ds(pl.multiple_of(j * step, step), step), n * channels : (n + 1) * channels] = kept.astype(BF)
        return carry

    def copy(i, k):
        to = lax.rem(me + k, owners)
        return pltpu.make_async_remote_copy(
            src_ref=send.at[i, pl.ds(pl.multiple_of(to * capacity, 16), capacity), :],
            dst_ref=recv.at[i, pl.ds(pl.multiple_of(me * capacity, 16), capacity), :],
            send_sem=send_sem.at[i, k],
            recv_sem=recv_sem.at[i, k],
            device_id={"shot": to},
            device_id_type=pl.DeviceIdType.MESH,
        )

    def chunk_one(i, carry):
        later = (i + chunks - 1) // chunks
        last = i // (chunks - 1)
        lax.fori_loop(tiles * i + later, tiles * (i + 1) + 1 - last, spread, 0)
        lax.fori_loop(i * (span // step), (i + 1) * (span // step), block_one, 0)
        at = pl.ds(pl.multiple_of(i * span, span), span)
        send[i] = nt_dot(pick[...], clean[at, :]).astype(BF)
        for k in range(1, owners):
            copy(i, k).start()
        own = pl.ds(pl.multiple_of(me * capacity, 16), capacity)
        recv[i, own, :] = send[i, own, :]
        return carry

    pl.semaphore_wait(barrier, owners - 1)
    lax.fori_loop(0, chunks, chunk_one, 0)

    step_two = STEP_TWO
    blocks_two = samples // step_two
    bank_two = tau_two.shape[0]
    depth_two = 5 * step_two
    cells_win[0] = jnp.zeros((depth_two, width), BF)
    cells_win[blocks_two + 1] = jnp.zeros((depth_two, width), BF)
    ids = lax.broadcasted_iota(jnp.int32, (rows, width), 0)
    for b in [2] if aligned else range(5):
        place[0 if aligned else b] = jnp.where(ids == spot_ref[b : b + 1, :], 1.0, 0.0).astype(BF)
    out_id = lax.broadcasted_iota(jnp.int32, (width, 1), 0)
    origin = (out_id % folds) * fold_lanes + out_id // folds
    lane = lax.broadcasted_iota(jnp.int32, (width, width), 1)
    perm[...] = jnp.where(origin == lane, 1.0, 0.0).astype(BF)
    per_two = 128 // step_two

    def assemble(i, tile):
        turned = recv[i, :, tile * 128 : (tile + 1) * 128].astype(F32).T.astype(BF)
        at = pl.ds((i * tiles + tile) * per_two + 1, per_two)
        if aligned:
            cells = jnp.dot(turned, place[0], preferred_element_type=F32).astype(BF)
            cells = cells.reshape(per_two, step_two, width)
            for b in range(5):
                gap = (b - 2) * fold_lanes
                lo, hi = max(0, -gap), width - max(0, gap)
                r = slice(b * step_two, (b + 1) * step_two)
                cells_win[at, r, lo:hi] = cells[:, :, lo + gap : hi + gap]
                if lo > 0:
                    cells_win[at, r, 0:lo] = jnp.zeros((per_two, step_two, lo), BF)
                if hi < width:
                    cells_win[at, r, hi:width] = jnp.zeros((per_two, step_two, width - hi), BF)
        else:
            for b in range(5):
                cells = jnp.dot(turned, place[b], preferred_element_type=F32).astype(BF)
                cells_win[at, b * step_two : (b + 1) * step_two, :] = cells.reshape(per_two, step_two, width)

    def block_two(j, carry):
        for g in range(width // 256):
            lanes = slice(g * 256, (g + 1) * 256)
            stack = cells_win[pl.ds(j, 3), :, lanes].reshape(3 * depth_two, 256)
            filtered = jnp.dot(band_two[...], stack, preferred_element_type=F32)
            noise = shrink(filtered, tau_two, bank_two, step_two)
            centre = cells_win[j + 1, 2 * step_two : 3 * step_two, lanes].astype(F32)
            mask = jnp.where(spot_ref[2:3, lanes] >= 0, 1.0, 0.0)
            at = pl.ds(pl.multiple_of(j * step_two, step_two), step_two)
            done[at, lanes] = ((centre - noise) * mask).astype(BF)
        return carry

    def restore(m, carry):
        at = pl.ds(pl.multiple_of(m * span, span), span)
        turned = nt_dot(perm[...], done[at, :])
        out_ref[:, :, at] = turned.reshape(fold_lanes, folds, span).astype(BF)
        return carry

    def chunk_two(i, carry):
        later = (i + chunks - 1) // chunks
        last = i // (chunks - 1)
        for k in range(1, owners):
            copy(i, k).wait_recv()
        for tile in range(tiles):
            assemble(i, tile)
        count = span // step_two
        lax.fori_loop(i * count - later, (i + 1) * count - 1 + last, block_two, 0)
        lax.fori_loop(i - later, i + last, restore, 0)
        return carry

    lax.fori_loop(0, chunks, chunk_two, 0)

    def finish(i, carry):
        for k in range(1, owners):
            copy(i, k).wait_send()
        return carry

    lax.fori_loop(0, chunks, finish, 0)


def vmem():
    return pl.BlockSpec(memory_space=pltpu.VMEM)


def smem():
    return pl.BlockSpec(memory_space=pltpu.SMEM)


def per_device(
    data, live_mask, patch_start, receiver_slot, shot_kernels, shot_tau, receiver_kernels, receiver_tau
):
    _, lines, channels, samples = data.shape
    stations = receiver_slot.shape[1]
    shots = patch_start.shape[0]
    owners = lax.axis_size("shot")
    slots = stations // owners
    me = lax.axis_index("shot")
    first_line = lax.axis_index("line") * lines
    ends = lax.axis_size("line") - 1
    fold_lanes = lines * slots
    width = shots * fold_lanes

    mask = live_mask[0]
    live = data[0] * mask[..., None].astype(BF)
    top = lax.ppermute(live[lines - 1 :], "line", [(i, i + 1) for i in range(ends)])
    bottom = lax.ppermute(live[:1], "line", [(i + 1, i) for i in range(ends)])

    starts = lax.dynamic_slice_in_dim(patch_start, first_line, lines, 1)
    own_starts = lax.dynamic_slice_in_dim(starts, me, 1, 0)[0]
    own_slots = jnp.concatenate(
        [lax.dynamic_slice(receiver_slot, (n, own_starts[n]), (1, channels)) for n in range(lines)], axis=0
    )
    owner = (own_slots // slots).reshape(-1)
    line_ids = jnp.arange(lines, dtype=jnp.int32)[:, None]
    place = (line_ids * slots + own_slots % slots).reshape(-1)
    slot_ids = me * slots + jnp.arange(slots, dtype=jnp.int32)
    hits = receiver_slot[:, None, :] == slot_ids[None, :, None]
    station = jnp.sum(jnp.where(hits, jnp.arange(stations, dtype=jnp.int32), 0), axis=-1)
    channel = station[None] - starts[:, :, None]
    covered = (channel >= 0) & (channel < channels)
    covered = covered.reshape(shots, fold_lanes)
    lower = jnp.asarray(np.tril(np.ones((shots, shots), np.int32), -1))
    fold = jnp.sum(lower[:, :, None] * covered[None].astype(jnp.int32), axis=1)
    fold_ids = jnp.arange(shots, dtype=jnp.int32)[:, None, None]
    takes = covered[None] & (fold[None] == fold_ids)
    shot_ids = jnp.arange(shots, dtype=jnp.int32)[:, None]

    band_one = band_matrix(shot_kernels, STEP_ONE, 2)
    band_two = band_matrix(receiver_kernels, STEP_TWO, 3)
    blocks = samples // STEP_ONE
    copies = 1 if fold_lanes % 128 == 0 else 5
    weights = mask.astype(F32)

    def places(size):
        rows = (owner * size + place).reshape(1, lines * channels)
        source = shot_ids * size + jnp.arange(fold_lanes, dtype=jnp.int32)[None]
        spot = (jnp.sum(jnp.where(takes, source[None] + 1, 0), axis=1) - 1).reshape(width)
        padded = jnp.pad(spot, (2 * fold_lanes, 2 * fold_lanes), constant_values=-1)
        spots = jnp.stack([padded[b * fold_lanes : b * fold_lanes + width] for b in range(5)])
        return rows, spots

    rows, spots = places(fold_lanes)

    def run(size, ident, rows, spots):
        total = owners * size
        return pl.pallas_call(
            functools.partial(bank_kernel, shots),
            out_shape=jax.ShapeDtypeStruct((fold_lanes, shots, samples), BF),
            in_specs=[vmem()] * 7 + [smem(), vmem(), smem()],
            out_specs=vmem(),
            scratch_shapes=[
                pltpu.VMEM((blocks + 1, (lines + 2) * 5 * STEP_ONE, channels), BF),
                pltpu.VMEM((samples, lines * channels), BF),
                pltpu.VMEM((total, lines * channels), BF),
                pltpu.VMEM((CHUNKS, total, samples // CHUNKS), BF),
                pltpu.VMEM((CHUNKS, total, samples // CHUNKS), BF),
                pltpu.VMEM((samples // STEP_TWO + 2, 5 * STEP_TWO, width), BF),
                pltpu.VMEM((samples, width), BF),
                pltpu.VMEM((copies, total, width), BF),
                pltpu.VMEM((width, width), BF),
                pltpu.SemaphoreType.DMA((CHUNKS, owners)),
                pltpu.SemaphoreType.DMA((CHUNKS, owners)),
            ],
            compiler_params=pltpu.CompilerParams(
                vmem_limit_bytes=VMEM, collective_id=ident, has_side_effects=True
            ),
            name="banks",
        )(live, top, bottom, weights, rows, spots, band_one, shot_tau, band_two, receiver_tau)

    out = run(fold_lanes, 0, rows, spots)
    return out.reshape(lines, slots, shots, samples)


def solution(mesh):
    return jax.shard_map(
        per_device,
        mesh=mesh,
        in_specs=(
            P("shot", "line", None, None),
            P("shot", "line", None),
            P(),
            P("line", None),
            P(),
            P(),
            P(),
            P(),
        ),
        out_specs=P("line", "shot", None, None),
        check_vma=False,
    )
```
